128 devices in a mesh: kva: 8 (over y, x_hi), kvb: 16 (over x_lo, z, core).
Axes of the slice: x: 4 (x_hi: 2, x_lo: 2; x = x_hi * 2 + x_lo), y: 4, z: 4, core: 2. Of those that a mesh axis runs over, the one named last changes fastest.
Arguments:
- latent_cache: bfloat16 [2, 786432, 576], P(None, ('kva', 'kvb')), may hold values from -5 to 5
- lengths: int32 [2], replicated, may hold values from 196608 to 786432, as said below
- queries: bfloat16 [2, 2, 128, 576], replicated, may hold values from -24 to 24
- residual_in: bfloat16 [4, 7168], replicated, may hold values from -6 to 6
- value_up: bfloat16 [128, 512, 128], P(('kva', 'kvb')), may hold values from -0.25 to 0.25
- out_weight: bfloat16 [16384, 7168], P(('kva', 'kvb')), may hold values from -0.1875 to 0.1875
- norm_gain: bfloat16 [7168], replicated, may hold values from 0.5 to 1.5
- gate_weight: bfloat16 [7168, 18432], P(None, ('kva', 'kvb')), may hold values from -0.0625 to 0.0625
- up_weight: bfloat16 [7168, 18432], P(None, ('kva', 'kvb')), may hold values from -0.0625 to 0.0625
- down_weight: bfloat16 [18432, 7168], P(('kva', 'kvb')), may hold values from -0.15625 to 0.15625
Outputs:
- head_values: bfloat16 [4, 16384], P(None, ('kva', 'kvb'))
- mixed: bfloat16 [4, 7168], P(None, ('kva', 'kvb'))
The draws below stay inside these ranges and needn't reach their ends.
Inputs may be any that keep to these rules, and one draw needn't show every extreme that they name: `lengths`: each length is a multiple of 256; in every draw one request's length is exactly 786432.
All inputs are finite; a program needn't handle non-finite values.
Results may differ from the reference program's by a relative error of at most 0.02.
Values may be sent and summed in bfloat16 or wider, within the bound.
A program may use at most 128 MiB of HBM per device.

```python
import jax
import jax.numpy as jnp
from jax import lax

D = 7168
LAT = 512
ROPE = 64
NOPE = 128
VDIM = 128
FF = 18432
REQS = 2
NQ = 2
BLOCK = 256
CACHE_DEV = 6144
HEADS = 128
SEQ = 786432
ROWS = 4


def shared_lengths(key):
    key = jax.random.fold_in(key, 11)
    full_blocks = SEQ // BLOCK
    block_counts = jax.random.randint(key, (REQS,), full_blocks // 4, full_blocks + 1)
    full_one = jax.random.randint(jax.random.fold_in(key, 1), (), 0, REQS)
    block_counts = jnp.where(jnp.arange(REQS) == full_one, full_blocks, block_counts)
    return (block_counts * BLOCK).astype(jnp.int32)


def shared_anchors(key):
    lengths = shared_lengths(key)
    key = jax.random.fold_in(key, 12)
    last_row = jnp.clip(jax.random.normal(jax.random.fold_in(key, 4), (REQS, LAT + ROPE), jnp.float32), -4.0, 4.0)
    return (lengths, last_row)


def draw_lengths(key, part):
    return shared_lengths(key)


def draw_latent_cache(key, part):
    lengths, last_row = shared_anchors(key)
    key = jax.random.fold_in(key, 21)
    request_ids = jnp.arange(REQS)
    latent_rows = jnp.clip(jax.random.normal(key, (REQS, SEQ, LAT + ROPE), jnp.float32), -5.0, 5.0)
    latent_rows = latent_rows.at[request_ids, lengths - 1].set(last_row)
    return latent_rows.astype(jnp.bfloat16)


def draw_queries(key, part):
    lengths, last_row = shared_anchors(key)
    key = jax.random.fold_in(key, 31)
    query_spread = 6.0 * ((NOPE + ROPE) / (LAT + ROPE)) ** 0.5
    head_kind = jax.random.randint(jax.random.fold_in(key, 1), (REQS, NQ, HEADS), 0, 8)
    drawn_rows = jnp.clip(query_spread * jax.random.normal(key, (REQS, NQ, HEADS, LAT + ROPE), jnp.float32), -20.0, 20.0)
    strength = jax.random.uniform(jax.random.fold_in(key, 2), (REQS, NQ, HEADS), jnp.float32, 0.6, 1.5)
    drawn_rows = jnp.where((head_kind == 1)[..., None], strength[..., None] * last_row[:, None, None, :], drawn_rows)
    return drawn_rows.astype(jnp.bfloat16)


def spiked(result, stream_key, source, target, shards_of, factor):
    owner, partner = [(jnp.arange(result.shape[axis_at]) // (result.shape[axis_at] // shards_of)).reshape([-1 if axis == axis_at else 1 for axis in range(result.ndim)]) for axis_at in (source, target)]
    chosen = jax.random.permutation(stream_key, shards_of)[partner]
    strong = (owner == chosen) | (owner == (partner + shards_of // 2) % shards_of)
    return jnp.where(strong, factor * result, result)


def level_of(own_key, extent, shards, low, top_value):
    def one(axis_at, parts):
        heights = jax.random.uniform(jax.random.fold_in(jax.random.fold_in(own_key, 6), axis_at), (parts,), jnp.float32, low / len(shards), top_value / len(shards))
        return jnp.repeat(jnp.exp(heights), extent[axis_at] // parts).reshape((-1,) + (1,) * (len(extent) - axis_at - 1))

    loudness = one(*shards[0])
    for cut in shards[1:]:
        loudness = loudness * one(*cut)
    return loudness


def gaussian(key, extent, deviation, most, shards=(), kind=jnp.bfloat16):
    factor_of = level_of(key, extent, shards, -0.22, 0.18) if shards else 1.0
    result = jax.random.normal(key, extent, jnp.float32) * deviation * factor_of
    return jnp.minimum(jnp.maximum(result, -most), most).astype(kind)


def bell_draw_with(rng, shape, scale, most, pieces, heavy, kind=jnp.bfloat16):
    drawn = scale * jax.random.normal(rng, shape, jnp.float32)
    if pieces:
        drawn = drawn * level_of(rng, shape, pieces, -0.22, 0.18)
    return jnp.clip(spiked(drawn, jax.random.fold_in(rng, 3), *heavy), -most, most).astype(kind)


def setup_inputs(seed: int = 0) -> dict:
    arg_keys = jax.random.split(jax.random.key(seed), 11)
    return {
        "latent_cache": draw_latent_cache(jax.random.fold_in(arg_keys[10], 71), 0),
        "lengths": draw_lengths(jax.random.fold_in(arg_keys[10], 71), 0),
        "queries": draw_queries(jax.random.fold_in(arg_keys[10], 71), 0),
        "residual_in": gaussian(arg_keys[3], (ROWS, D), 1.0, 6.0),
        "value_up": gaussian(arg_keys[4], (HEADS, LAT, VDIM), LAT ** -0.5, 0.25, ((0, 128),)),
        "out_weight": bell_draw_with(arg_keys[5], (HEADS * VDIM, D), (HEADS * VDIM) ** -0.5, 0.1875, ((0, 128),), (0, 1, 128, 5.5)),
        "norm_gain": jnp.clip(1.0 + 0.1 * jax.random.normal(arg_keys[6], (D,), jnp.float32), 0.5, 1.5).astype(jnp.bfloat16),
        "gate_weight": gaussian(arg_keys[7], (D, FF), D ** -0.5, 0.0625, ((1, 128),)),
        "up_weight": gaussian(arg_keys[8], (D, FF), D ** -0.5, 0.0625, ((1, 128),)),
        "down_weight": bell_draw_with(arg_keys[9], (FF, D), FF ** -0.5, 0.15625, ((0, 128),), (0, 1, 128, 5.5)),
    }


def reference(latent_cache, lengths, queries, residual_in, value_up, out_weight, norm_gain, gate_weight, up_weight, down_weight):
    score_scale = (NOPE + ROPE) ** (-0.5)
    visible = lengths[:, None] - NQ + 1 + jnp.arange(NQ, dtype=jnp.int32)[None, :]
    query_wide = queries.astype(jnp.float32)

    def visit(carry_now, seg_index):
        offset = (seg_index * CACHE_DEV).astype(jnp.int32)
        window = lax.dynamic_slice_in_dim(latent_cache, offset, CACHE_DEV, 1)
        wide_rows = window.astype(jnp.float32)
        scores = jnp.einsum('rjhc,rpc->rjhp', query_wide, wide_rows) * score_scale
        positions = offset + jnp.arange(CACHE_DEV, dtype=jnp.int32)
        usable = (positions[None, None, :] < visible[:, :, None])[:, :, None, :]
        seg_max = lax.optimization_barrier(jnp.max(jnp.where(usable, scores, -1e+30), axis=-1))
        weights = jnp.where(usable, jnp.exp(scores - seg_max[..., None]), 0.0).astype(jnp.bfloat16)
        seg_total = lax.optimization_barrier(jnp.sum(weights.astype(jnp.float32), axis=-1))
        seg_numer = jnp.einsum('rjhp,rpc->rjhc', weights.astype(jnp.float32), wide_rows[:, :, :LAT])
        divisor = jnp.maximum(seg_total, 1.0)
        seg_out = (seg_numer / divisor[..., None]).astype(jnp.bfloat16)
        seg_lse = seg_max + jnp.log(divisor)
        return (carry_now, (seg_out, seg_lse))
    start_carry = jnp.zeros((), jnp.float32)
    end_carry, stacked = lax.scan(visit, start_carry, jnp.arange(SEQ // CACHE_DEV, dtype=jnp.int32))
    seg_outs, seg_lses = stacked
    top_lse = lax.optimization_barrier(jnp.max(seg_lses, axis=0))
    factor = jnp.exp(seg_lses - top_lse[None])
    numer_sum = lax.optimization_barrier(jnp.sum(factor[..., None] * seg_outs.astype(jnp.float32), axis=0))
    denom_sum = lax.optimization_barrier(jnp.sum(factor, axis=0))
    attention = (numer_sum / denom_sum[..., None]).astype(jnp.bfloat16)
    head_values = jnp.einsum('rjhc,hce->rjhe', attention.astype(jnp.float32), value_up.astype(jnp.float32))
    head_values = head_values.astype(jnp.bfloat16).reshape(ROWS, HEADS * VDIM)
    projection = jnp.dot(head_values, out_weight, preferred_element_type=jnp.float32)
    attended = (residual_in.astype(jnp.float32) + projection).astype(jnp.bfloat16)
    wide_att = attended.astype(jnp.float32)
    mean_square = lax.optimization_barrier(jnp.sum(wide_att * wide_att, axis=-1)) / D
    normed = (wide_att * lax.rsqrt(mean_square + 1e-06)[:, None] * norm_gain.astype(jnp.float32)).astype(jnp.bfloat16)
    gate_part = jnp.dot(normed, gate_weight, preferred_element_type=jnp.float32)
    up_part = jnp.dot(normed, up_weight, preferred_element_type=jnp.float32)
    hidden = (jax.nn.silu(gate_part) * up_part).astype(jnp.bfloat16)
    mixed = (wide_att + jnp.dot(hidden, down_weight, preferred_element_type=jnp.float32)).astype(jnp.bfloat16)
    return (head_values, mixed)
```

```python
import functools
import math

import jax
import jax.numpy as jnp
from jax import lax
from jax.experimental import pallas as pl
from jax.experimental.pallas import tpu as pltpu
from jax.sharding import PartitionSpec as P

ROPE = 64
NOPE = 128
SCALE = (NOPE + ROPE) ** (-0.5)
NEG = -1e30
CHUNK = 1024
BF = jnp.bfloat16
F32 = jnp.float32
NT = (((1,), (1,)), ((), ()))
MESH = pl.DeviceIdType.MESH


def split3(x):
    hi = x.astype(BF).astype(F32)
    rest = x - hi
    mid = rest.astype(BF).astype(F32)
    return hi, mid, (rest - mid).astype(BF).astype(F32)


def kernel(
    na,
    nb,
    lengths,
    cache,
    queries,
    residual,
    value_up,
    out_w,
    gain,
    gate_w,
    up_w,
    down_w,
    hv_out,
    mix_out,
    kbuf,
    qbuf,
    sbuf,
    resbuf,
    vbuf,
    owbuf,
    gainbuf,
    gbuf,
    ubuf,
    dbuf,
    msg1,
    rcv1,
    x2,
    msg2,
    rcv2,
    stack,
    msg3,
    rcv3,
    msg4,
    rcv4,
    msg5,
    rcv5,
    wide,
    msg6,
    rcv6,
    msg7,
    rcv7,
    ksem,
    wsem,
    ssem,
    rsem,
):
    a = lax.axis_index("kva")
    b = lax.axis_index("kvb")
    requests, width, rows = kbuf.shape
    nq, heads = qbuf.shape[1], qbuf.shape[3]
    latent = vbuf.shape[1]
    qrows = nq * heads
    tokens = requests * nq
    d_model = owbuf.shape[1]
    block = d_model // na
    tiles = block // 128
    group = heads // na
    pieces = latent // 128
    chunks = rows // CHUNK
    ext = latent + 128

    def peer_a(k):
        return lax.rem(a + k, na)

    def peer_b(k):
        return lax.rem(b + k, nb)

    qcopy = pltpu.make_async_copy(queries, qbuf, wsem.at[0])
    qcopy.start()
    kcopies = []
    for r in range(requests):
        for c in range(chunks):
            part = pl.ds(c * CHUNK, CHUNK)
            copy = pltpu.make_async_copy(
                cache.at[r, :, part], kbuf.at[r, :, part], ksem.at[r * chunks + c]
            )
            copy.start()
            kcopies.append(copy)
    barrier = pltpu.get_barrier_semaphore()
    for k in range(1, na):
        pl.semaphore_signal(barrier, inc=1, device_id=(peer_a(k), b), device_id_type=MESH)
    for k in range(1, nb):
        pl.semaphore_signal(barrier, inc=1, device_id=(a, peer_b(k)), device_id_type=MESH)
    weights = [
        pltpu.make_async_copy(src, dst, wsem.at[i + 1])
        for i, (src, dst) in enumerate(
            (
                (value_up, vbuf),
                (out_w, owbuf),
                (residual, resbuf),
                (gain, gainbuf),
                (gate_w, gbuf),
                (up_w, ubuf),
                (down_w, dbuf),
            )
        )
    ]

    def send(stage, src, dst, device):
        pltpu.make_async_remote_copy(
            src_ref=src,
            dst_ref=dst,
            send_sem=ssem.at[stage],
            recv_sem=rsem.at[stage],
            device_id=device,
            device_id_type=MESH,
        ).start()

    def arrived(stage, buf):
        pltpu.make_async_copy(buf, buf, rsem.at[stage]).wait()

    def sent(stage, buf):
        pltpu.make_async_copy(buf, buf, ssem.at[stage]).wait()

    first = (a * nb + b) * rows
    factor = SCALE * math.log2(math.e)
    qcopy.wait()
    for r in range(requests):
        q = jnp.concatenate([qbuf[r, j].T for j in range(nq)], axis=0)
        peak = None
        for c in range(chunks):
            part = pl.ds(c * CHUNK, CHUNK)
            kcopies[r * chunks + c].wait()
            s = jnp.dot(q, kbuf[r, :, part], preferred_element_type=F32)
            pos = first + c * CHUNK + lax.broadcasted_iota(jnp.int32, (1, CHUNK), 1)
            halves = []
            for j in range(nq):
                bias = jnp.where(pos < lengths[r] - (nq - 1) + j, 0.0, NEG)
                halves.append(s[j * heads : (j + 1) * heads] + bias)
            s = jnp.concatenate(halves, axis=0)
            sbuf[:, part] = s
            for t in range(CHUNK // 128):
                tile = s[:, t * 128 : (t + 1) * 128]
                peak = tile if peak is None else jnp.maximum(peak, tile)
        if r == 0:
            for copy in weights:
                copy.start()
        top = jnp.max(peak, axis=1, keepdims=True)
        shift = top * factor
        total = jnp.zeros((qrows, 128), F32)
        numer = jnp.zeros((qrows, latent), F32)
        for c in range(chunks):
            part = pl.ds(c * CHUNK, CHUNK)
            w = jnp.exp2(sbuf[:, part] * factor - shift)
            for t in range(CHUNK // 128):
                total = total + w[:, t * 128 : (t + 1) * 128]
            numer = numer + lax.dot_general(
                w.astype(BF), kbuf[r, :latent, part], NT, preferred_element_type=F32
            )
        total = jnp.sum(total, axis=1, keepdims=True)
        lse = top * SCALE + jnp.log(total)
        out = (numer * (1.0 / total)).astype(BF)
        lane = lax.broadcasted_iota(jnp.int32, (1, 128), 1)
        hi, mid, lo = split3(lse)
        tail = jnp.where(lane == 0, hi, jnp.where(lane == 1, mid, jnp.where(lane == 2, lo, 0.0)))
        msg1[r, :, :, :latent] = out.reshape(nq, heads, latent)
        msg1[r, :, :, latent:] = tail.astype(BF).reshape(nq, heads, 128)
        if r == 0:
            pl.semaphore_wait(barrier, na + nb - 2)
        for k in range(1, na):
            p = peer_a(k)
            send(
                r,
                msg1.at[r, :, pl.ds(pl.multiple_of(p * group, group), group), :],
                rcv1.at[r, k - 1],
                (p, b),
            )

    for r in range(requests):
        arrived(r, rcv1.at[r])
        mine = msg1[r, :, pl.ds(pl.multiple_of(a * group, group), group), :]
        parts = [mine] + [rcv1[r, k] for k in range(na - 1)]
        for j in range(nq):
            vals = [x[j, :, :latent].astype(F32) for x in parts]
            tails = [x[j, :, latent:].astype(F32) for x in parts]
            lses = [jnp.sum(t, axis=1, keepdims=True) for t in tails]
            top = functools.reduce(jnp.maximum, lses)
            ws = [jnp.exp(x - top) for x in lses]
            den = functools.reduce(jnp.add, ws)
            num = functools.reduce(jnp.add, [w * v for w, v in zip(ws, vals)])
            val = num * (1.0 / den)
            lse = top + jnp.log(den)
            rj = r * nq + j
            for c in range(pieces):
                x2[:, c * tokens + rj, :] = val[:, c * 128 : (c + 1) * 128]
            for c, piece in enumerate(split3(jnp.broadcast_to(lse, (group, 128)))):
                x2[:, (pieces + c) * tokens + rj, :] = piece
    for c in range((pieces + 3) * tokens, x2.shape[1]):
        x2[:, c, :] = jnp.zeros((group, 128), F32)
    msg2[...] = x2[...].astype(BF)
    for k in range(1, nb):
        p = peer_b(k)
        send(2, msg2.at[p], rcv2.at[k - 1], (a, p))

    arrived(2, rcv2)
    parts = [msg2[b].astype(F32)] + [rcv2[k].astype(F32) for k in range(nb - 1)]
    edge = pieces * tokens
    lses = [
        x[edge : edge + tokens] + x[edge + tokens : edge + 2 * tokens] + x[edge + 2 * tokens : edge + 3 * tokens]
        for x in parts
    ]
    top = functools.reduce(jnp.maximum, lses)
    ws = [jnp.exp(x - top) for x in lses]
    den = 1.0 / functools.reduce(jnp.add, ws)
    for copy in weights[:1]:
        copy.wait()
    head_values = jnp.zeros((tokens, 128), F32)
    for c in range(pieces):
        num = functools.reduce(
            jnp.add, [w * x[c * tokens : (c + 1) * tokens] for w, x in zip(ws, parts)]
        )
        head_values = head_values + jnp.dot(
            (num * den).astype(BF), vbuf[0, c * 128 : (c + 1) * 128, :], preferred_element_type=F32
        )
    head_values = head_values.astype(BF)
    hv_out[...] = head_values

    def scatter(stage, lhs, wbuf, msg, rcv):
        for k in range(1, na + 1):
            p = peer_a(k)
            y = jnp.dot(
                lhs,
                wbuf[:, pl.ds(pl.multiple_of(p * block, 128), block)],
                preferred_element_type=F32,
            )
            for t in range(tiles):
                stack[k - 1, t * tokens : (t + 1) * tokens, :] = y[:, t * 128 : (t + 1) * 128]
            if k < na:
                msg[k - 1] = stack[k - 1].astype(BF)
                send(stage, msg.at[k - 1], rcv.at[k - 1], (p, b))
        arrived(stage, rcv)
        return functools.reduce(
            jnp.add, [stack[na - 1]] + [rcv[k].astype(F32) for k in range(na - 1)]
        )

    def spread(stage, x, msg, rcv):
        msg[...] = x.astype(BF)
        for k in range(1, nb):
            send(stage, msg, rcv.at[k - 1], (a, peer_b(k)))
        arrived(stage, rcv)
        return functools.reduce(jnp.add, [x] + [rcv[k].astype(F32) for k in range(nb - 1)])

    for copy in weights[1:]:
        copy.wait()
    stack[...] = jnp.zeros(stack.shape, F32)
    summed = spread(4, scatter(3, head_values, owbuf, msg3, rcv3), msg4, rcv4)
    for t in range(tiles):
        stack[0, t * tokens : (t + 1) * tokens, :] = resbuf[
            :, pl.ds(pl.multiple_of(a * block + t * 128, 128), 128)
        ].astype(F32)
    attended = (stack[0] + summed).astype(BF)
    msg5[...] = attended
    for k in range(1, na):
        send(5, msg5, rcv5.at[k - 1], (peer_a(k), b))
    attended = attended.astype(F32)
    arrived(5, rcv5)
    for k in range(na):
        p = lax.rem(a - k + na, na)
        x = attended if k == 0 else rcv5[k - 1].astype(F32)
        for t in range(tiles):
            wide[:, pl.ds(pl.multiple_of(p * block + t * 128, 128), 128)] = x[
                t * tokens : (t + 1) * tokens
            ]
    att = wide[...]
    mean_square = jnp.sum(att * att, axis=1, keepdims=True) / d_model
    normed = (
        att * lax.rsqrt(mean_square + 1e-06) * gainbuf[...].astype(F32).reshape(1, d_model)
    ).astype(BF)
    gate = lax.dot_general(normed, gbuf[...], NT, preferred_element_type=F32)
    up = lax.dot_general(normed, ubuf[...], NT, preferred_element_type=F32)
    hidden = (gate / (1.0 + jnp.exp(-gate)) * up).astype(BF)
    ffn = spread(7, scatter(6, hidden, dbuf, msg6, rcv6), msg7, rcv7)
    mixed = (attended + ffn).astype(BF).astype(F32)

    own = mix_out.shape[1]
    picked = jnp.zeros((tokens, own), F32)
    for t in range(tiles):
        row = t * 128 + lax.broadcasted_iota(jnp.int32, (128, own), 0)
        col = b * own + lax.broadcasted_iota(jnp.int32, (128, own), 1)
        pick = jnp.where(row == col, 1.0, 0.0).astype(BF)
        picked = picked + jnp.dot(
            mixed[t * tokens : (t + 1) * tokens].astype(BF), pick, preferred_element_type=F32
        )
    mix_out[...] = picked.astype(BF)

    for r in range(requests):
        sent(r, rcv1.at[r])
    for stage, buf in ((2, rcv2), (3, rcv3), (4, rcv4), (5, rcv5), (6, rcv6), (7, rcv7)):
        sent(stage, buf)


def per_device(
    na,
    nb,
    latent_cache,
    lengths,
    queries,
    residual_in,
    value_up,
    out_weight,
    norm_gain,
    gate_weight,
    up_weight,
    down_weight,
):
    latent_cache = jnp.swapaxes(latent_cache, 1, 2)
    queries = jnp.swapaxes(queries, 2, 3)
    gate_weight = gate_weight.T
    up_weight = up_weight.T
    rows = latent_cache.shape[2]
    requests, nq, _, heads = queries.shape
    latent = value_up.shape[1]
    tokens, d_model = residual_in.shape
    group = heads // na
    ext = latent + 128
    lines = 32
    chunks = rows // CHUNK
    vmem = pltpu.VMEM
    scratch = [
        vmem(latent_cache.shape, BF),
        vmem(queries.shape, BF),
        vmem((nq * heads, rows), F32),
        vmem(residual_in.shape, BF),
        vmem(value_up.shape, BF),
        vmem(out_weight.shape, BF),
        vmem(norm_gain.shape, BF),
        vmem(gate_weight.shape, BF),
        vmem(up_weight.shape, BF),
        vmem(down_weight.shape, BF),
        vmem((requests, nq, heads, ext), BF),
        vmem((requests, na - 1, nq, group, ext), BF),
        vmem((group, lines, 128), F32),
        vmem((group, lines, 128), BF),
        vmem((nb - 1, lines, 128), BF),
        vmem((na, lines, 128), F32),
        vmem((na - 1, lines, 128), BF),
        vmem((na - 1, lines, 128), BF),
        vmem((lines, 128), BF),
        vmem((nb - 1, lines, 128), BF),
        vmem((lines, 128), BF),
        vmem((na - 1, lines, 128), BF),
        vmem((tokens, d_model), F32),
        vmem((na - 1, lines, 128), BF),
        vmem((na - 1, lines, 128), BF),
        vmem((lines, 128), BF),
        vmem((nb - 1, lines, 128), BF),
        pltpu.SemaphoreType.DMA((requests * chunks,)),
        pltpu.SemaphoreType.DMA((8,)),
        pltpu.SemaphoreType.DMA((8,)),
        pltpu.SemaphoreType.DMA((8,)),
    ]
    anywhere = pl.BlockSpec(memory_space=pl.ANY)
    return pl.pallas_call(
        functools.partial(kernel, na, nb),
        out_shape=(
            jax.ShapeDtypeStruct((tokens, value_up.shape[0] * value_up.shape[2]), BF),
            jax.ShapeDtypeStruct((tokens, d_model // (na * nb)), BF),
        ),
        in_specs=[pl.BlockSpec(memory_space=pltpu.SMEM)] + [anywhere] * 9,
        out_specs=(pl.BlockSpec(memory_space=pltpu.VMEM), pl.BlockSpec(memory_space=pltpu.VMEM)),
        scratch_shapes=scratch,
        compiler_params=pltpu.CompilerParams(
            collective_id=0, has_side_effects=True, vmem_limit_bytes=60 * 1024 * 1024
        ),
    )(
        lengths,
        latent_cache,
        queries,
        residual_in,
        value_up,
        out_weight,
        norm_gain,
        gate_weight,
        up_weight,
        down_weight,
    )


def solution(mesh):
    na, nb = mesh.shape["kva"], mesh.shape["kvb"]
    both = ("kva", "kvb")
    in_specs = (
        P(None, both, None),
        P(),
        P(),
        P(),
        P(both, None, None),
        P(both, None),
        P(),
        P(None, both),
        P(None, both),
        P(both, None),
    )
    out_specs = (P(None, both), P(None, both))
    return jax.shard_map(
        functools.partial(per_device, na, nb),
        mesh=mesh,
        in_specs=in_specs,
        out_specs=out_specs,
        check_vma=False,
    )
```

```python
import math

import jax
import jax.numpy as jnp
from jax import lax
from jax.experimental import pallas as pl
from jax.experimental.pallas import tpu as pltpu
from jax.sharding import PartitionSpec as P

ROPE = 64
NOPE = 128
SCALE = (NOPE + ROPE) ** (-0.5)
NEG = -1e30
CHUNK = 1024
BF = jnp.bfloat16
F32 = jnp.float32
NT = (((1,), (1,)), ((), ()))
MESH = pl.DeviceIdType.MESH


def split3(x):
    hi = x.astype(BF).astype(F32)
    rest = x - hi
    mid = rest.astype(BF).astype(F32)
    return hi, mid, (rest - mid).astype(BF).astype(F32)


def farthest_first():
    hops = lambda o: sum(min(v, 4 - v) for v in o)
    offsets = [(y, x, z) for y in range(4) for x in range(4) for z in range(4)]
    return sorted(offsets, key=hops, reverse=True)[:-1]


def kernel(
    lengths,
    cache,
    queries,
    residual,
    value_up,
    out_w,
    gain,
    gate_w,
    up_w,
    down_w,
    hv_out,
    mix_out,
    kbuf,
    qbuf,
    sbuf,
    resbuf,
    vbuf,
    owbuf,
    gainbuf,
    gbuf,
    ubuf,
    dbuf,
    msg1,
    rcv1,
    x2,
    msg2,
    rcv2,
    stack,
    resid,
    msg3,
    rcv3,
    msg4,
    rcv4,
    wide,
    msg5,
    rcv5,
    msg6,
    rcv6,
    ksem,
    wsem,
    ssem,
    rsem,
):
    a = lax.axis_index("kva")
    b = lax.axis_index("kvb")
    requests, width, rows = kbuf.shape
    nq, heads = qbuf.shape[1], qbuf.shape[3]
    latent = vbuf.shape[1]
    qrows = nq * heads
    tokens = requests * nq
    d_model = owbuf.shape[1]
    tiles = d_model // 128
    chips = heads // 2
    pieces = latent // 128
    chunks = rows // CHUNK
    own = mix_out.shape[1]

    core = b % 2
    ys = [(a // 2 + k) % 4 for k in range(4)]
    xs = [((a % 2) * 2 + b // 8 + k) % 4 for k in range(4)]
    zs = [((b // 2) % 4 + k) % 4 for k in range(4)]
    chip = ys[0] * 16 + xs[0] * 4 + zs[0]
    y_part = [y * 2 for y in ys]
    x_part = [x // 2 for x in xs]
    x_low = [(x % 2) * 8 + core for x in xs]
    z_part = [z * 2 for z in zs]
    sibling = (a, b + 1 - 2 * core)

    def device_at(dy, dx, dz):
        return (y_part[dy] + x_part[dx], x_low[dx] + z_part[dz])

    def chip_at(dy, dx, dz):
        return ys[dy] * 16 + xs[dx] * 4 + zs[dz]

    offsets = farthest_first()

    qcopy = pltpu.make_async_copy(queries, qbuf, wsem.at[0])
    qcopy.start()
    kcopies = []
    for r in range(requests):
        for c in range(chunks):
            part = pl.ds(c * CHUNK, CHUNK)
            copy = pltpu.make_async_copy(
                cache.at[r, :, part], kbuf.at[r, :, part], ksem.at[r * chunks + c]
            )
            copy.start()
            kcopies.append(copy)
    weights = [
        pltpu.make_async_copy(src, dst, wsem.at[i + 1])
        for i, (src, dst) in enumerate(
            (
                (value_up, vbuf),
                (residual, resbuf),
                (out_w, owbuf),
                (gain, gainbuf),
                (gate_w, gbuf),
                (up_w, ubuf),
                (down_w, dbuf),
            )
        )
    ]
    barrier = pltpu.get_barrier_semaphore()
    pl.semaphore_signal(barrier, inc=1, device_id=sibling, device_id_type=MESH)
    for off in offsets:
        pl.semaphore_signal(barrier, inc=1, device_id=device_at(*off), device_id_type=MESH)

    def send(stage, src, dst, device):
        pltpu.make_async_remote_copy(
            src_ref=src,
            dst_ref=dst,
            send_sem=ssem.at[stage],
            recv_sem=rsem.at[stage],
            device_id=device,
            device_id_type=MESH,
        ).start()

    def arrived(stage, buf):
        pltpu.make_async_copy(buf, buf, rsem.at[stage]).wait()

    def sent(stage, buf):
        pltpu.make_async_copy(buf, buf, ssem.at[stage]).wait()

    first = (a * 16 + b) * rows
    factor = SCALE * math.log2(math.e)

    def scores(r):
        at = lax.broadcasted_iota(jnp.int32, (heads, heads), 0)
        head = lax.broadcasted_iota(jnp.int32, (heads, heads), 1)
        order = jnp.where(head == (at % chips) * 2 + at // chips, 1.0, 0.0).astype(BF)
        q = jnp.concatenate(
            [
                lax.dot_general(order, qbuf[r, j], NT, preferred_element_type=F32).astype(BF)
                for j in range(nq)
            ],
            axis=0,
        )
        peak = None
        for c in range(chunks):
            part = pl.ds(c * CHUNK, CHUNK)
            kcopies[r * chunks + c].wait()
            s = jnp.dot(q, kbuf[r, :, part], preferred_element_type=F32)
            pos = first + c * CHUNK + lax.broadcasted_iota(jnp.int32, (1, CHUNK), 1)
            halves = []
            for j in range(nq):
                bias = jnp.where(pos < lengths[r] - (nq - 1) + j, 0.0, NEG)
                halves.append(s[j * heads : (j + 1) * heads] + bias)
            s = jnp.concatenate(halves, axis=0)
            sbuf[:, part] = s
            for t in range(CHUNK // 128):
                tile = s[:, t * 128 : (t + 1) * 128]
                peak = tile if peak is None else jnp.maximum(peak, tile)
        return jnp.max(peak, axis=1, keepdims=True)

    def values(r, top):
        shift = top * factor
        total = jnp.zeros((qrows, 128), F32)
        numer = jnp.zeros((qrows, latent), F32)
        for c in range(chunks):
            part = pl.ds(c * CHUNK, CHUNK)
            w = jnp.exp2(sbuf[:, part] * factor - shift)
            for t in range(CHUNK // 128):
                total = total + w[:, t * 128 : (t + 1) * 128]
            numer = numer + lax.dot_general(
                w.astype(BF), kbuf[r, :latent, part], NT, preferred_element_type=F32
            )
        total = jnp.sum(total, axis=1, keepdims=True)
        lse = top * SCALE + jnp.log(total)
        out = (numer * (1.0 / total)).astype(BF)
        lane = lax.broadcasted_iota(jnp.int32, (1, 128), 1)
        hi, mid, lo = split3(lse)
        tail = jnp.where(lane == 0, hi, jnp.where(lane == 1, mid, jnp.where(lane == 2, lo, 0.0)))
        tail = tail.astype(BF)
        for half in range(2):
            for j in range(nq):
                at = slice(j * heads + half * chips, j * heads + (half + 1) * chips)
                msg1[r, half, j, :, :latent] = out[at]
                msg1[r, half, j, :, latent:] = tail[at]
        if r == 0:
            pl.semaphore_wait(barrier, len(offsets) + 1)
        send(r, msg1.at[r, 1 - core], rcv1.at[r], sibling)

    def exchange(r):
        arrived(r, rcv1.at[r])
        for j in range(nq):
            parts = [msg1[r, core, j], rcv1[r, j]]
            vals = [x[:, :latent].astype(F32) for x in parts]
            lses = [jnp.sum(x[:, latent:].astype(F32), axis=1, keepdims=True) for x in parts]
            top = jnp.maximum(*lses)
            ws = [jnp.exp(x - top) for x in lses]
            den = ws[0] + ws[1]
            val = (ws[0] * vals[0] + ws[1] * vals[1]) * (1.0 / den)
            lse = top + jnp.log(den)
            for c in range(pieces):
                x2[:, c * nq + j, :] = val[:, c * 128 : (c + 1) * 128]
            for c, piece in enumerate(split3(jnp.broadcast_to(lse, (chips, 128)))):
                x2[:, (pieces + c) * nq + j, :] = piece
        msg2[r] = x2[...].astype(BF)
        for k, off in enumerate(offsets):
            send(2 + r, msg2.at[r, chip_at(*off)], rcv2.at[r, k], device_at(*off))

    def head_rows(r):
        arrived(2 + r, rcv2.at[r, pl.ds(0, len(offsets))])
        rcv2[r, len(offsets)] = msg2[r, chip]
        x = rcv2[r].astype(F32)
        edge = pieces * nq
        lse = (
            x[:, edge : edge + nq]
            + x[:, edge + nq : edge + 2 * nq]
            + x[:, edge + 2 * nq : edge + 3 * nq]
        )
        top = jnp.max(lse, axis=0, keepdims=True)
        w = jnp.exp(lse - top)
        w = w * (1.0 / jnp.sum(w, axis=0, keepdims=True))
        w = jnp.concatenate([w] * pieces, axis=1)
        att = jnp.sum(w * x[:, :edge], axis=0)
        total = jnp.zeros((nq, 128), F32)
        for c in range(pieces):
            total = total + jnp.dot(
                att[c * nq : (c + 1) * nq].astype(BF),
                vbuf[0, c * 128 : (c + 1) * 128, :],
                preferred_element_type=F32,
            )
        return total

    for c in range((pieces + 3) * nq, x2.shape[1]):
        x2[:, c, :] = jnp.zeros((chips, 128), F32)
    qcopy.wait()
    top = scores(0)
    for copy in weights:
        copy.start()
    values(0, top)
    top = scores(1)
    exchange(0)
    values(1, top)
    exchange(1)
    for copy in weights:
        copy.wait()
    for t in range(tiles):
        resid[t * tokens : (t + 1) * tokens, :] = resbuf[:, t * 128 : (t + 1) * 128].astype(F32)
    head_values = jnp.concatenate([head_rows(0), head_rows(1)], axis=0).astype(BF)
    hv_out[...] = head_values

    y = jnp.dot(head_values, owbuf[...], preferred_element_type=F32)
    for t in range(tiles):
        stack[t * tokens : (t + 1) * tokens, :] = y[:, t * 128 : (t + 1) * 128]
    msg3[...] = stack[...].astype(BF)
    send(4, msg3, rcv3, sibling)
    arrived(4, rcv3)
    summed = stack[...] + rcv3[...].astype(F32)
    lines = tiles * tokens
    third = (lines // 3 + 15) // 16 * 16
    for step in range(3):
        msg4[step] = summed.astype(BF)
        for k in (2, 1, 3):
            for g in range(3):
                part = pl.ds(g * third, min(third, lines - g * third))
                off = [0, 0, 0]
                off[(g + step) % 3] = k
                send(
                    5 + step,
                    msg4.at[step, part, :],
                    rcv4.at[step, k - 1, part, :],
                    device_at(*off),
                )
        arrived(5 + step, rcv4.at[step])
        for k in range(3):
            summed = summed + rcv4[step, k].astype(F32)
    stack[...] = (resid[...] + summed).astype(BF).astype(F32)
    for t in range(tiles):
        wide[:, t * 128 : (t + 1) * 128] = stack[t * tokens : (t + 1) * tokens, :]
    att = wide[...]
    mean_square = jnp.sum(att * att, axis=1, keepdims=True) / d_model
    normed = (
        att * lax.rsqrt(mean_square + 1e-06) * gainbuf[...].astype(F32).reshape(1, d_model)
    ).astype(BF)
    gate = lax.dot_general(normed, gbuf[...], NT, preferred_element_type=F32)
    up = lax.dot_general(normed, ubuf[...], NT, preferred_element_type=F32)
    hidden = (gate / (1.0 + jnp.exp(-gate)) * up).astype(BF)

    y = jnp.dot(hidden, dbuf[...], preferred_element_type=F32)
    y = y + jnp.where(chip * 2 + core == 0, att, 0.0)
    y = jnp.concatenate([y, jnp.zeros((tokens, 128), F32)], axis=1)
    for o in range(2 * chips):
        msg5[o % 2, o // 2] = y[:, o * own : o * own + 128]
    send(8, msg5.at[1 - core], rcv5, sibling)
    arrived(8, rcv5)
    msg6[...] = msg5[core] + rcv5[...]
    for k, off in enumerate(offsets):
        send(9, msg6.at[chip_at(*off)], rcv6.at[k], device_at(*off))
    arrived(9, rcv6)
    total = msg6[chip] + jnp.sum(rcv6[...], axis=0)
    mix_out[...] = total[:, :own].astype(BF)

    for r in range(requests):
        sent(r, rcv1.at[r])
        sent(2 + r, rcv2.at[r, pl.ds(0, len(offsets))])
    sent(4, rcv3)
    for step in range(3):
        sent(5 + step, rcv4.at[step])
    sent(8, rcv5)
    sent(9, rcv6)


def per_device(
    latent_cache,
    lengths,
    queries,
    residual_in,
    value_up,
    out_weight,
    norm_gain,
    gate_weight,
    up_weight,
    down_weight,
):
    latent_cache = jnp.swapaxes(latent_cache, 1, 2)
    queries = jnp.swapaxes(queries, 2, 3)
    gate_weight = gate_weight.T
    up_weight = up_weight.T
    rows = latent_cache.shape[2]
    requests, nq, _, heads = queries.shape
    latent = value_up.shape[1]
    tokens, d_model = residual_in.shape
    chips = heads // 2
    lines = tokens * d_model // 128
    vmem = pltpu.VMEM
    scratch = [
        vmem(latent_cache.shape, BF),
        vmem(queries.shape, BF),
        vmem((nq * heads, rows), F32),
        vmem(residual_in.shape, BF),
        vmem(value_up.shape, BF),
        vmem(out_weight.shape, BF),
        vmem(norm_gain.shape, BF),
        vmem(gate_weight.shape, BF),
        vmem(up_weight.shape, BF),
        vmem(down_weight.shape, BF),
        vmem((requests, 2, nq, chips, latent + 128), BF),
        vmem((requests, nq, chips, latent + 128), BF),
        vmem((chips, 16, 128), F32),
        vmem((requests, chips, 16, 128), BF),
        vmem((requests, chips, 16, 128), BF),
        vmem((lines, 128), F32),
        vmem((lines, 128), F32),
        vmem((lines, 128), BF),
        vmem((lines, 128), BF),
        vmem((3, lines, 128), BF),
        vmem((3, 3, lines, 128), BF),
        vmem((tokens, d_model), F32),
        vmem((2, chips, tokens, 128), F32),
        vmem((chips, tokens, 128), F32),
        vmem((chips, tokens, 128), F32),
        vmem((chips - 1, tokens, 128), F32),
        pltpu.SemaphoreType.DMA((requests * (rows // CHUNK),)),
        pltpu.SemaphoreType.DMA((8,)),
        pltpu.SemaphoreType.DMA((10,)),
        pltpu.SemaphoreType.DMA((10,)),
    ]
    anywhere = pl.BlockSpec(memory_space=pl.ANY)
    return pl.pallas_call(
        kernel,
        out_shape=(
            jax.ShapeDtypeStruct((tokens, value_up.shape[0] * value_up.shape[2]), BF),
            jax.ShapeDtypeStruct((tokens, d_model // heads), BF),
        ),
        in_specs=[pl.BlockSpec(memory_space=pltpu.SMEM)] + [anywhere] * 9,
        out_specs=(pl.BlockSpec(memory_space=pltpu.VMEM), pl.BlockSpec(memory_space=pltpu.VMEM)),
        scratch_shapes=scratch,
        compiler_params=pltpu.CompilerParams(
            collective_id=0, has_side_effects=True, vmem_limit_bytes=60 * 1024 * 1024
        ),
    )(
        lengths,
        latent_cache,
        queries,
        residual_in,
        value_up,
        out_weight,
        norm_gain,
        gate_weight,
        up_weight,
        down_weight,
    )


def solution(mesh):
    both = ("kva", "kvb")
    in_specs = (
        P(None, both, None),
        P(),
        P(),
        P(),
        P(both, None, None),
        P(both, None),
        P(),
        P(None, both),
        P(None, both),
        P(both, None),
    )
    out_specs = (P(None, both), P(None, both))
    return jax.shard_map(
        per_device,
        mesh=mesh,
        in_specs=in_specs,
        out_specs=out_specs,
        check_vma=False,
    )
```

```python
import math

import jax
import jax.numpy as jnp
from jax import lax
from jax.experimental import pallas as pl
from jax.experimental.pallas import tpu as pltpu
from jax.sharding import PartitionSpec as P

ROPE = 64
NOPE = 128
SCALE = (NOPE + ROPE) ** (-0.5)
NEG = -1e30
CHUNK = 1024
AHEAD = 2
BF = jnp.bfloat16
F32 = jnp.float32
NT = (((1,), (1,)), ((), ()))
MESH = pl.DeviceIdType.MESH


def split3(x):
    hi = x.astype(BF).astype(F32)
    rest = x - hi
    mid = rest.astype(BF).astype(F32)
    return hi, mid, (rest - mid).astype(BF).astype(F32)


def farthest_first():
    hops = lambda o: sum(min(v, 4 - v) for v in o)
    offsets = [(y, x, z) for y in range(4) for x in range(4) for z in range(4)]
    return sorted(offsets, key=hops, reverse=True)[:-1]


def kernel(
    lengths,
    cache,
    queries,
    residual,
    value_up,
    out_w,
    gain,
    gate_w,
    up_w,
    down_w,
    hv_out,
    mix_out,
    kbuf,
    qbuf,
    sbuf,
    resbuf,
    vbuf,
    owbuf,
    gainbuf,
    gbuf,
    ubuf,
    dbuf,
    msg1,
    rcv1,
    x2,
    msg2,
    rcv2,
    stack,
    resid,
    msg3,
    rcv3,
    msg4,
    rcv4,
    wide,
    msg5,
    rcv5,
    msg6,
    rcv6,
    ksem,
    wsem,
    ssem,
    rsem,
):
    a = lax.axis_index("kva")
    b = lax.axis_index("kvb")
    requests, width, rows = kbuf.shape
    nq, heads = qbuf.shape[1], qbuf.shape[3]
    latent = vbuf.shape[1]
    qrows = nq * heads
    tokens = requests * nq
    d_model = owbuf.shape[1]
    tiles = d_model // 128
    chips = heads // 2
    pieces = latent // 128
    chunks = rows // CHUNK
    own = mix_out.shape[1]

    core = b % 2
    ys = [(a // 2 + k) % 4 for k in range(4)]
    xs = [((a % 2) * 2 + b // 8 + k) % 4 for k in range(4)]
    zs = [((b // 2) % 4 + k) % 4 for k in range(4)]
    chip = ys[0] * 16 + xs[0] * 4 + zs[0]
    y_part = [y * 2 for y in ys]
    x_part = [x // 2 for x in xs]
    x_low = [(x % 2) * 8 + core for x in xs]
    z_part = [z * 2 for z in zs]
    sibling = (a, b + 1 - 2 * core)

    def device_at(dy, dx, dz):
        return (y_part[dy] + x_part[dx], x_low[dx] + z_part[dz])

    def chip_at(dy, dx, dz):
        return ys[dy] * 16 + xs[dx] * 4 + zs[dz]

    offsets = farthest_first()

    qcopy = pltpu.make_async_copy(queries, qbuf, wsem.at[0])
    qcopy.start()
    kcopies = []
    for r in range(requests):
        for c in range(chunks):
            part = pl.ds(c * CHUNK, CHUNK)
            kcopies.append(
                pltpu.make_async_copy(
                    cache.at[r, :, part], kbuf.at[r, :, part], ksem.at[r * chunks + c]
                )
            )
    for copy in kcopies[:AHEAD]:
        copy.start()
    weights = [
        pltpu.make_async_copy(src, dst, wsem.at[i + 1])
        for i, (src, dst) in enumerate(
            (
                (value_up, vbuf),
                (residual, resbuf),
                (out_w, owbuf),
                (gain, gainbuf),
                (gate_w, gbuf),
                (up_w, ubuf),
                (down_w, dbuf),
            )
        )
    ]
    barrier = pltpu.get_barrier_semaphore()
    pl.semaphore_signal(barrier, inc=1, device_id=sibling, device_id_type=MESH)
    for off in offsets:
        pl.semaphore_signal(barrier, inc=1, device_id=device_at(*off), device_id_type=MESH)

    def send(stage, src, dst, device):
        pltpu.make_async_remote_copy(
            src_ref=src,
            dst_ref=dst,
            send_sem=ssem.at[stage],
            recv_sem=rsem.at[stage],
            device_id=device,
            device_id_type=MESH,
        ).start()

    def arrived(stage, buf):
        pltpu.make_async_copy(buf, buf, rsem.at[stage]).wait()

    def sent(stage, buf):
        pltpu.make_async_copy(buf, buf, ssem.at[stage]).wait()

    first = (a * 16 + b) * rows
    factor = SCALE * math.log2(math.e)

    def scores(r):
        at = lax.broadcasted_iota(jnp.int32, (heads, heads), 0)
        head = lax.broadcasted_iota(jnp.int32, (heads, heads), 1)
        order = jnp.where(head == (at % chips) * 2 + at // chips, 1.0, 0.0).astype(BF)
        q = jnp.concatenate(
            [
                lax.dot_general(order, qbuf[r, j], NT, preferred_element_type=F32).astype(BF)
                for j in range(nq)
            ],
            axis=0,
        )
        peak = None
        for c in range(chunks):
            part = pl.ds(c * CHUNK, CHUNK)
            kcopies[r * chunks + c].wait()
            if r == 0:
                kcopies[c + AHEAD].start()
            s = jnp.dot(q, kbuf[r, :, part], preferred_element_type=F32)
            pos = first + c * CHUNK + lax.broadcasted_iota(jnp.int32, (1, CHUNK), 1)
            halves = []
            for j in range(nq):
                bias = jnp.where(pos < lengths[r] - (nq - 1) + j, 0.0, NEG)
                halves.append(s[j * heads : (j + 1) * heads] + bias)
            s = jnp.concatenate(halves, axis=0)
            sbuf[:, part] = s
            for t in range(CHUNK // 128):
                tile = s[:, t * 128 : (t + 1) * 128]
                peak = tile if peak is None else jnp.maximum(peak, tile)
        return jnp.max(peak, axis=1, keepdims=True)

    def values(r, top):
        shift = top * factor
        total = jnp.zeros((qrows, 128), F32)
        numer = jnp.zeros((qrows, latent), F32)
        for c in range(chunks):
            part = pl.ds(c * CHUNK, CHUNK)
            if r == 0 and c < chunks - AHEAD:
                kcopies[chunks + AHEAD + c].start()
            w = jnp.exp2(sbuf[:, part] * factor - shift)
            for t in range(CHUNK // 128):
                total = total + w[:, t * 128 : (t + 1) * 128]
            numer = numer + lax.dot_general(
                w.astype(BF), kbuf[r, :latent, part], NT, preferred_element_type=F32
            )
        total = jnp.sum(total, axis=1, keepdims=True)
        lse = top * SCALE + jnp.log(total)
        out = (numer * (1.0 / total)).astype(BF)
        lane = lax.broadcasted_iota(jnp.int32, (1, 128), 1)
        hi, mid, lo = split3(lse)
        tail = jnp.where(lane == 0, hi, jnp.where(lane == 1, mid, jnp.where(lane == 2, lo, 0.0)))
        tail = tail.astype(BF)
        for half in range(2):
            for j in range(nq):
                at = slice(j * heads + half * chips, j * heads + (half + 1) * chips)
                msg1[r, half, j, :, :latent] = out[at]
                msg1[r, half, j, :, latent:] = tail[at]
        if r == 0:
            pl.semaphore_wait(barrier, len(offsets) + 1)
        send(r, msg1.at[r, 1 - core], rcv1.at[r], sibling)

    def exchange(r):
        arrived(r, rcv1.at[r])
        for j in range(nq):
            parts = [msg1[r, core, j], rcv1[r, j]]
            vals = [x[:, :latent].astype(F32) for x in parts]
            lses = [jnp.sum(x[:, latent:].astype(F32), axis=1, keepdims=True) for x in parts]
            top = jnp.maximum(*lses)
            ws = [jnp.exp(x - top) for x in lses]
            den = ws[0] + ws[1]
            val = (ws[0] * vals[0] + ws[1] * vals[1]) * (1.0 / den)
            lse = top + jnp.log(den)
            for c in range(pieces):
                x2[:, c * nq + j, :] = val[:, c * 128 : (c + 1) * 128]
            for c, piece in enumerate(split3(jnp.broadcast_to(lse, (chips, 128)))):
                x2[:, (pieces + c) * nq + j, :] = piece
        msg2[r] = x2[...].astype(BF)
        for k, off in enumerate(offsets):
            send(2 + r, msg2.at[r, chip_at(*off)], rcv2.at[r, k], device_at(*off))

    def head_rows(r):
        arrived(2 + r, rcv2.at[r, pl.ds(0, len(offsets))])
        rcv2[r, len(offsets)] = msg2[r, chip]
        x = rcv2[r].astype(F32)
        edge = pieces * nq
        lse = (
            x[:, edge : edge + nq]
            + x[:, edge + nq : edge + 2 * nq]
            + x[:, edge + 2 * nq : edge + 3 * nq]
        )
        top = jnp.max(lse, axis=0, keepdims=True)
        w = jnp.exp(lse - top)
        w = w * (1.0 / jnp.sum(w, axis=0, keepdims=True))
        w = jnp.concatenate([w] * pieces, axis=1)
        att = jnp.sum(w * x[:, :edge], axis=0)
        total = jnp.zeros((nq, 128), F32)
        for c in range(pieces):
            total = total + jnp.dot(
                att[c * nq : (c + 1) * nq].astype(BF),
                vbuf[0, c * 128 : (c + 1) * 128, :],
                preferred_element_type=F32,
            )
        return total

    for c in range((pieces + 3) * nq, x2.shape[1]):
        x2[:, c, :] = jnp.zeros((chips, 128), F32)
    qcopy.wait()
    values(0, scores(0))
    top = scores(1)
    for copy in weights:
        copy.start()
    exchange(0)
    values(1, top)
    exchange(1)
    for copy in weights:
        copy.wait()
    for t in range(tiles):
        resid[t * tokens : (t + 1) * tokens, :] = resbuf[:, t * 128 : (t + 1) * 128].astype(F32)
    head_values = jnp.concatenate([head_rows(0), head_rows(1)], axis=0).astype(BF)
    hv_out[...] = head_values

    y = jnp.dot(head_values, owbuf[...], preferred_element_type=F32)
    for t in range(tiles):
        stack[t * tokens : (t + 1) * tokens, :] = y[:, t * 128 : (t + 1) * 128]
    msg3[...] = stack[...].astype(BF)
    send(4, msg3, rcv3, sibling)
    arrived(4, rcv3)
    summed = stack[...] + rcv3[...].astype(F32)
    lines = tiles * tokens
    third = (lines // 3 + 15) // 16 * 16
    for step in range(3):
        msg4[step] = summed.astype(BF)
        for k in (2, 1, 3):
            for g in range(3):
                part = pl.ds(g * third, min(third, lines - g * third))
                off = [0, 0, 0]
                off[(g + step) % 3] = k
                send(
                    5 + step,
                    msg4.at[step, part, :],
                    rcv4.at[step, k - 1, part, :],
                    device_at(*off),
                )
        arrived(5 + step, rcv4.at[step])
        for k in range(3):
            summed = summed + rcv4[step, k].astype(F32)
    stack[...] = (resid[...] + summed).astype(BF).astype(F32)
    for t in range(tiles):
        wide[:, t * 128 : (t + 1) * 128] = stack[t * tokens : (t + 1) * tokens, :]
    att = wide[...]
    mean_square = jnp.sum(att * att, axis=1, keepdims=True) / d_model
    normed = (
        att * lax.rsqrt(mean_square + 1e-06) * gainbuf[...].astype(F32).reshape(1, d_model)
    ).astype(BF)
    gate = lax.dot_general(normed, gbuf[...], NT, preferred_element_type=F32)
    up = lax.dot_general(normed, ubuf[...], NT, preferred_element_type=F32)
    hidden = (gate / (1.0 + jnp.exp(-gate)) * up).astype(BF)

    y = jnp.dot(hidden, dbuf[...], preferred_element_type=F32)
    y = y + jnp.where(chip * 2 + core == 0, att, 0.0)
    y = jnp.concatenate([y, jnp.zeros((tokens, 128), F32)], axis=1)
    for o in range(2 * chips):
        msg5[o % 2, o // 2] = y[:, o * own : o * own + 128]
    send(8, msg5.at[1 - core], rcv5, sibling)
    arrived(8, rcv5)
    msg6[...] = msg5[core] + rcv5[...]
    for k, off in enumerate(offsets):
        send(9, msg6.at[chip_at(*off)], rcv6.at[k], device_at(*off))
    arrived(9, rcv6)
    total = msg6[chip] + jnp.sum(rcv6[...], axis=0)
    mix_out[...] = total[:, :own].astype(BF)

    for r in range(requests):
        sent(r, rcv1.at[r])
        sent(2 + r, rcv2.at[r, pl.ds(0, len(offsets))])
    sent(4, rcv3)
    for step in range(3):
        sent(5 + step, rcv4.at[step])
    sent(8, rcv5)
    sent(9, rcv6)


def hand_on(head_values, mixed, head_values_out, mixed_out, sems):
    copies = [
        pltpu.make_async_copy(head_values, head_values_out, sems.at[0]),
        pltpu.make_async_copy(mixed, mixed_out, sems.at[1]),
    ]
    for copy in copies:
        copy.start()
    for copy in copies:
        copy.wait()


def per_device(
    latent_cache,
    lengths,
    queries,
    residual_in,
    value_up,
    out_weight,
    norm_gain,
    gate_weight,
    up_weight,
    down_weight,
):
    latent_cache = jnp.swapaxes(latent_cache, 1, 2)
    queries = jnp.swapaxes(queries, 2, 3)
    gate_weight = gate_weight.T
    up_weight = up_weight.T
    rows = latent_cache.shape[2]
    requests, nq, _, heads = queries.shape
    latent = value_up.shape[1]
    tokens, d_model = residual_in.shape
    chips = heads // 2
    lines = tokens * d_model // 128
    vmem = pltpu.VMEM
    scratch = [
        vmem(latent_cache.shape, BF),
        vmem(queries.shape, BF),
        vmem((nq * heads, rows), F32),
        vmem(residual_in.shape, BF),
        vmem(value_up.shape, BF),
        vmem(out_weight.shape, BF),
        vmem(norm_gain.shape, BF),
        vmem(gate_weight.shape, BF),
        vmem(up_weight.shape, BF),
        vmem(down_weight.shape, BF),
        vmem((requests, 2, nq, chips, latent + 128), BF),
        vmem((requests, nq, chips, latent + 128), BF),
        vmem((chips, 16, 128), F32),
        vmem((requests, chips, 16, 128), BF),
        vmem((requests, chips, 16, 128), BF),
        vmem((lines, 128), F32),
        vmem((lines, 128), F32),
        vmem((lines, 128), BF),
        vmem((lines, 128), BF),
        vmem((3, lines, 128), BF),
        vmem((3, 3, lines, 128), BF),
        vmem((tokens, d_model), F32),
        vmem((2, chips, tokens, 128), F32),
        vmem((chips, tokens, 128), F32),
        vmem((chips, tokens, 128), F32),
        vmem((chips - 1, tokens, 128), F32),
        pltpu.SemaphoreType.DMA((requests * (rows // CHUNK),)),
        pltpu.SemaphoreType.DMA((8,)),
        pltpu.SemaphoreType.DMA((10,)),
        pltpu.SemaphoreType.DMA((10,)),
    ]
    anywhere = pl.BlockSpec(memory_space=pl.ANY)
    results = pl.pallas_call(
        kernel,
        out_shape=(
            jax.ShapeDtypeStruct((tokens, value_up.shape[0] * value_up.shape[2]), BF),
            jax.ShapeDtypeStruct((tokens, d_model // heads), BF),
        ),
        in_specs=[pl.BlockSpec(memory_space=pltpu.SMEM)] + [anywhere] * 9,
        out_specs=(pl.BlockSpec(memory_space=pltpu.VMEM), pl.BlockSpec(memory_space=pltpu.VMEM)),
        scratch_shapes=scratch,
        compiler_params=pltpu.CompilerParams(
            collective_id=0, has_side_effects=True, vmem_limit_bytes=60 * 1024 * 1024
        ),
    )(
        lengths,
        latent_cache,
        queries,
        residual_in,
        value_up,
        out_weight,
        norm_gain,
        gate_weight,
        up_weight,
        down_weight,
    )
    return pl.pallas_call(
        hand_on,
        out_shape=tuple(jax.ShapeDtypeStruct(x.shape, x.dtype) for x in results),
        in_specs=[anywhere] * 2,
        out_specs=(anywhere,) * 2,
        scratch_shapes=[pltpu.SemaphoreType.DMA((2,))],
    )(*results)


def solution(mesh):
    both = ("kva", "kvb")
    in_specs = (
        P(None, both, None),
        P(),
        P(),
        P(),
        P(both, None, None),
        P(both, None),
        P(),
        P(None, both),
        P(None, both),
        P(both, None),
    )
    out_specs = (P(None, both), P(None, both))
    return jax.shard_map(
        per_device,
        mesh=mesh,
        in_specs=in_specs,
        out_specs=out_specs,
        check_vma=False,
    )
```

```python
import math

import jax
import jax.numpy as jnp
from jax import lax
from jax.experimental import pallas as pl
from jax.experimental.pallas import tpu as pltpu
from jax.sharding import PartitionSpec as P

ROPE = 64
NOPE = 128
SCALE = (NOPE + ROPE) ** (-0.5)
NEG = -1e30
CHUNK = 1024
WIDE = 3072
AHEAD = 2
BF = jnp.bfloat16
F32 = jnp.float32
NT = (((1,), (1,)), ((), ()))
MESH = pl.DeviceIdType.MESH


def split3(x):
    hi = x.astype(BF).astype(F32)
    rest = x - hi
    mid = rest.astype(BF).astype(F32)
    return hi, mid, (rest - mid).astype(BF).astype(F32)


def farthest_first():
    hops = lambda o: sum(min(v, 4 - v) for v in o)
    offsets = [(y, x, z) for y in range(4) for x in range(4) for z in range(4)]
    return sorted(offsets, key=hops, reverse=True)[:-1]


def kernel(
    lengths,
    cache,
    queries,
    residual,
    value_up,
    out_w,
    gain,
    gate_w,
    up_w,
    down_w,
    hv_out,
    mix_out,
    kbuf,
    qbuf,
    sbuf,
    resbuf,
    vbuf,
    owbuf,
    gainbuf,
    gbuf,
    ubuf,
    dbuf,
    msg1,
    rcv1,
    x2,
    msg2,
    rcv2,
    stack,
    resid,
    msg3,
    rcv3,
    msg4,
    rcv4,
    wide,
    msg5,
    rcv5,
    msg6,
    rcv6,
    ksem,
    wsem,
    ssem,
    rsem,
):
    a = lax.axis_index("kva")
    b = lax.axis_index("kvb")
    requests, width, rows = kbuf.shape
    nq, heads = qbuf.shape[1], qbuf.shape[3]
    latent = vbuf.shape[1]
    qrows = nq * heads
    tokens = requests * nq
    d_model = owbuf.shape[1]
    tiles = d_model // 128
    chips = heads // 2
    pieces = latent // 128
    chunks = rows // CHUNK
    own = mix_out.shape[1]

    core = b % 2
    ys = [(a // 2 + k) % 4 for k in range(4)]
    xs = [((a % 2) * 2 + b // 8 + k) % 4 for k in range(4)]
    zs = [((b // 2) % 4 + k) % 4 for k in range(4)]
    chip = ys[0] * 16 + xs[0] * 4 + zs[0]
    y_part = [y * 2 for y in ys]
    x_part = [x // 2 for x in xs]
    x_low = [(x % 2) * 8 + core for x in xs]
    z_part = [z * 2 for z in zs]
    sibling = (a, b + 1 - 2 * core)

    def device_at(dy, dx, dz):
        return (y_part[dy] + x_part[dx], x_low[dx] + z_part[dz])

    def chip_at(dy, dx, dz):
        return ys[dy] * 16 + xs[dx] * 4 + zs[dz]

    offsets = farthest_first()

    qcopy = pltpu.make_async_copy(queries, qbuf, wsem.at[0])
    qcopy.start()
    kcopies = []
    for r in range(requests):
        for c in range(chunks):
            part = pl.ds(c * CHUNK, CHUNK)
            kcopies.append(
                pltpu.make_async_copy(
                    cache.at[r, :, part], kbuf.at[r, :, part], ksem.at[r * chunks + c]
                )
            )
    for copy in kcopies[:AHEAD]:
        copy.start()
    weights = [
        pltpu.make_async_copy(src, dst, wsem.at[i + 1])
        for i, (src, dst) in enumerate(
            (
                (value_up, vbuf),
                (residual, resbuf),
                (out_w, owbuf),
                (gain, gainbuf),
                (gate_w, gbuf),
                (up_w, ubuf),
                (down_w, dbuf),
            )
        )
    ]
    barrier = pltpu.get_barrier_semaphore()
    pl.semaphore_signal(barrier, inc=1, device_id=sibling, device_id_type=MESH)
    for off in offsets:
        pl.semaphore_signal(barrier, inc=1, device_id=device_at(*off), device_id_type=MESH)

    def send(stage, src, dst, device):
        pltpu.make_async_remote_copy(
            src_ref=src,
            dst_ref=dst,
            send_sem=ssem.at[stage],
            recv_sem=rsem.at[stage],
            device_id=device,
            device_id_type=MESH,
        ).start()

    def arrived(stage, buf):
        pltpu.make_async_copy(buf, buf, rsem.at[stage]).wait()

    def sent(stage, buf):
        pltpu.make_async_copy(buf, buf, ssem.at[stage]).wait()

    first = (a * 16 + b) * rows
    factor = SCALE * math.log2(math.e)

    def scores(r):
        at = lax.broadcasted_iota(jnp.int32, (heads, heads), 0)
        head = lax.broadcasted_iota(jnp.int32, (heads, heads), 1)
        order = jnp.where(head == (at % chips) * 2 + at // chips, 1.0, 0.0).astype(BF)
        q = jnp.concatenate(
            [
                lax.dot_general(order, qbuf[r, j], NT, preferred_element_type=F32).astype(BF)
                for j in range(nq)
            ],
            axis=0,
        )
        peak = None
        span = CHUNK if r == 0 else WIDE
        for c in range(rows // span):
            part = pl.ds(c * span, span)
            at = r * chunks + c * span // CHUNK
            for copy in kcopies[at : at + span // CHUNK]:
                copy.wait()
            if r == 0:
                kcopies[c + AHEAD].start()
            s = jnp.dot(q, kbuf[r, :, part], preferred_element_type=F32)
            pos = first + c * span + lax.broadcasted_iota(jnp.int32, (1, span), 1)
            halves = []
            for j in range(nq):
                bias = jnp.where(pos < lengths[r] - (nq - 1) + j, 0.0, NEG)
                halves.append(s[j * heads : (j + 1) * heads] + bias)
            s = jnp.concatenate(halves, axis=0)
            sbuf[:, part] = s
            for t in range(span // 128):
                tile = s[:, t * 128 : (t + 1) * 128]
                peak = tile if peak is None else jnp.maximum(peak, tile)
        return jnp.max(peak, axis=1, keepdims=True)

    def values(r, top):
        shift = top * factor
        total = jnp.zeros((qrows, 128), F32)
        numer = jnp.zeros((qrows, latent), F32)
        span = CHUNK if r == 0 else WIDE
        for c in range(rows // span):
            part = pl.ds(c * span, span)
            if r == 0 and c < chunks - AHEAD:
                kcopies[chunks + AHEAD + c].start()
            w = jnp.exp2(sbuf[:, part] * factor - shift)
            for t in range(span // 128):
                total = total + w[:, t * 128 : (t + 1) * 128]
            numer = numer + lax.dot_general(
                w.astype(BF), kbuf[r, :latent, part], NT, preferred_element_type=F32
            )
        total = jnp.sum(total, axis=1, keepdims=True)
        lse = top * SCALE + jnp.log(total)
        out = (numer * (1.0 / total)).astype(BF)
        lane = lax.broadcasted_iota(jnp.int32, (1, 128), 1)
        hi, mid, lo = split3(lse)
        tail = jnp.where(lane == 0, hi, jnp.where(lane == 1, mid, jnp.where(lane == 2, lo, 0.0)))
        tail = tail.astype(BF)
        for half in range(2):
            for j in range(nq):
                at = slice(j * heads + half * chips, j * heads + (half + 1) * chips)
                msg1[r, half, j, :, :latent] = out[at]
                msg1[r, half, j, :, latent:] = tail[at]
        if r == 0:
            pl.semaphore_wait(barrier, len(offsets) + 1)
        send(r, msg1.at[r, 1 - core], rcv1.at[r], sibling)

    def exchange(r):
        arrived(r, rcv1.at[r])
        for j in range(nq):
            parts = [msg1[r, core, j], rcv1[r, j]]
            vals = [x[:, :latent].astype(F32) for x in parts]
            lses = [jnp.sum(x[:, latent:].astype(F32), axis=1, keepdims=True) for x in parts]
            top = jnp.maximum(*lses)
            ws = [jnp.exp(x - top) for x in lses]
            den = ws[0] + ws[1]
            val = (ws[0] * vals[0] + ws[1] * vals[1]) * (1.0 / den)
            lse = top + jnp.log(den)
            for c in range(pieces):
                x2[:, c * nq + j, :] = val[:, c * 128 : (c + 1) * 128]
            for c, piece in enumerate(split3(jnp.broadcast_to(lse, (chips, 128)))):
                x2[:, (pieces + c) * nq + j, :] = piece
        msg2[r] = x2[...].astype(BF)
        for k, off in enumerate(offsets):
            send(2 + r, msg2.at[r, chip_at(*off)], rcv2.at[r, k], device_at(*off))

    def head_rows(r):
        arrived(2 + r, rcv2.at[r, pl.ds(0, len(offsets))])
        rcv2[r, len(offsets)] = msg2[r, chip]
        x = rcv2[r].astype(F32)
        edge = pieces * nq
        lse = (
            x[:, edge : edge + nq]
            + x[:, edge + nq : edge + 2 * nq]
            + x[:, edge + 2 * nq : edge + 3 * nq]
        )
        top = jnp.max(lse, axis=0, keepdims=True)
        w = jnp.exp(lse - top)
        w = w * (1.0 / jnp.sum(w, axis=0, keepdims=True))
        w = jnp.concatenate([w] * pieces, axis=1)
        att = jnp.sum(w * x[:, :edge], axis=0)
        total = jnp.zeros((nq, 128), F32)
        for c in range(pieces):
            total = total + jnp.dot(
                att[c * nq : (c + 1) * nq].astype(BF),
                vbuf[0, c * 128 : (c + 1) * 128, :],
                preferred_element_type=F32,
            )
        return total

    for c in range((pieces + 3) * nq, x2.shape[1]):
        x2[:, c, :] = jnp.zeros((chips, 128), F32)
    qcopy.wait()
    values(0, scores(0))
    top = scores(1)
    for copy in weights:
        copy.start()
    exchange(0)
    values(1, top)
    exchange(1)
    for copy in weights:
        copy.wait()
    for t in range(tiles):
        resid[t * tokens : (t + 1) * tokens, :] = resbuf[:, t * 128 : (t + 1) * 128].astype(F32)
    head_values = jnp.concatenate([head_rows(0), head_rows(1)], axis=0).astype(BF)
    hv_out[...] = head_values

    y = jnp.dot(head_values, owbuf[...], preferred_element_type=F32)
    for t in range(tiles):
        stack[t * tokens : (t + 1) * tokens, :] = y[:, t * 128 : (t + 1) * 128]
    msg3[...] = stack[...].astype(BF)
    send(4, msg3, rcv3, sibling)
    arrived(4, rcv3)
    summed = stack[...] + rcv3[...].astype(F32)
    lines = tiles * tokens
    third = (lines // 3 + 15) // 16 * 16
    for step in range(3):
        msg4[step] = summed.astype(BF)
        for k in (2, 1, 3):
            for g in range(3):
                part = pl.ds(g * third, min(third, lines - g * third))
                off = [0, 0, 0]
                off[(g + step) % 3] = k
                send(
                    5 + step,
                    msg4.at[step, part, :],
                    rcv4.at[step, k - 1, part, :],
                    device_at(*off),
                )
        arrived(5 + step, rcv4.at[step])
        for k in range(3):
            summed = summed + rcv4[step, k].astype(F32)
    stack[...] = (resid[...] + summed).astype(BF).astype(F32)
    for t in range(tiles):
        wide[:, t * 128 : (t + 1) * 128] = stack[t * tokens : (t + 1) * tokens, :]
    att = wide[...]
    mean_square = jnp.sum(att * att, axis=1, keepdims=True) / d_model
    normed = (
        att * lax.rsqrt(mean_square + 1e-06) * gainbuf[...].astype(F32).reshape(1, d_model)
    ).astype(BF)
    gate = lax.dot_general(normed, gbuf[...], NT, preferred_element_type=F32)
    up = lax.dot_general(normed, ubuf[...], NT, preferred_element_type=F32)
    hidden = (gate / (1.0 + jnp.exp(-gate)) * up).astype(BF)

    y = jnp.dot(hidden, dbuf[...], preferred_element_type=F32)
    y = y + jnp.where(chip * 2 + core == 0, att, 0.0)
    y = jnp.concatenate([y, jnp.zeros((tokens, 128), F32)], axis=1)
    for o in range(2 * chips):
        msg5[o % 2, o // 2] = y[:, o * own : o * own + 128]
    send(8, msg5.at[1 - core], rcv5, sibling)
    arrived(8, rcv5)
    msg6[...] = msg5[core] + rcv5[...]
    for k, off in enumerate(offsets):
        send(9, msg6.at[chip_at(*off)], rcv6.at[k], device_at(*off))
    arrived(9, rcv6)
    total = msg6[chip] + jnp.sum(rcv6[...], axis=0)
    mix_out[...] = total[:, :own].astype(BF)

    for r in range(requests):
        sent(r, rcv1.at[r])
        sent(2 + r, rcv2.at[r, pl.ds(0, len(offsets))])
    sent(4, rcv3)
    for step in range(3):
        sent(5 + step, rcv4.at[step])
    sent(8, rcv5)
    sent(9, rcv6)


def hand_on(head_values, mixed, head_values_out, mixed_out, sems):
    copies = [
        pltpu.make_async_copy(head_values, head_values_out, sems.at[0]),
        pltpu.make_async_copy(mixed, mixed_out, sems.at[1]),
    ]
    for copy in copies:
        copy.start()
    for copy in copies:
        copy.wait()


def per_device(
    latent_cache,
    lengths,
    queries,
    residual_in,
    value_up,
    out_weight,
    norm_gain,
    gate_weight,
    up_weight,
    down_weight,
):
    latent_cache = jnp.swapaxes(latent_cache, 1, 2)
    queries = jnp.swapaxes(queries, 2, 3)
    gate_weight = gate_weight.T
    up_weight = up_weight.T
    rows = latent_cache.shape[2]
    requests, nq, _, heads = queries.shape
    latent = value_up.shape[1]
    tokens, d_model = residual_in.shape
    chips = heads // 2
    lines = tokens * d_model // 128
    vmem = pltpu.VMEM
    scratch = [
        vmem(latent_cache.shape, BF),
        vmem(queries.shape, BF),
        vmem((nq * heads, rows), F32),
        vmem(residual_in.shape, BF),
        vmem(value_up.shape, BF),
        vmem(out_weight.shape, BF),
        vmem(norm_gain.shape, BF),
        vmem(gate_weight.shape, BF),
        vmem(up_weight.shape, BF),
        vmem(down_weight.shape, BF),
        vmem((requests, 2, nq, chips, latent + 128), BF),
        vmem((requests, nq, chips, latent + 128), BF),
        vmem((chips, 16, 128), F32),
        vmem((requests, chips, 16, 128), BF),
        vmem((requests, chips, 16, 128), BF),
        vmem((lines, 128), F32),
        vmem((lines, 128), F32),
        vmem((lines, 128), BF),
        vmem((lines, 128), BF),
        vmem((3, lines, 128), BF),
        vmem((3, 3, lines, 128), BF),
        vmem((tokens, d_model), F32),
        vmem((2, chips, tokens, 128), F32),
        vmem((chips, tokens, 128), F32),
        vmem((chips, tokens, 128), F32),
        vmem((chips - 1, tokens, 128), F32),
        pltpu.SemaphoreType.DMA((requests * (rows // CHUNK),)),
        pltpu.SemaphoreType.DMA((8,)),
        pltpu.SemaphoreType.DMA((10,)),
        pltpu.SemaphoreType.DMA((10,)),
    ]
    anywhere = pl.BlockSpec(memory_space=pl.ANY)
    results = pl.pallas_call(
        kernel,
        out_shape=(
            jax.ShapeDtypeStruct((tokens, value_up.shape[0] * value_up.shape[2]), BF),
            jax.ShapeDtypeStruct((tokens, d_model // heads), BF),
        ),
        in_specs=[pl.BlockSpec(memory_space=pltpu.SMEM)] + [anywhere] * 9,
        out_specs=(pl.BlockSpec(memory_space=pltpu.VMEM), pl.BlockSpec(memory_space=pltpu.VMEM)),
        scratch_shapes=scratch,
        compiler_params=pltpu.CompilerParams(
            collective_id=0, has_side_effects=True, vmem_limit_bytes=60 * 1024 * 1024
        ),
    )(
        lengths,
        latent_cache,
        queries,
        residual_in,
        value_up,
        out_weight,
        norm_gain,
        gate_weight,
        up_weight,
        down_weight,
    )
    return pl.pallas_call(
        hand_on,
        out_shape=tuple(jax.ShapeDtypeStruct(x.shape, x.dtype) for x in results),
        in_specs=[anywhere] * 2,
        out_specs=(anywhere,) * 2,
        scratch_shapes=[pltpu.SemaphoreType.DMA((2,))],
    )(*results)


def solution(mesh):
    both = ("kva", "kvb")
    in_specs = (
        P(None, both, None),
        P(),
        P(),
        P(),
        P(both, None, None),
        P(both, None),
        P(),
        P(None, both),
        P(None, both),
        P(both, None),
    )
    out_specs = (P(None, both), P(None, both))
    return jax.shard_map(
        per_device,
        mesh=mesh,
        in_specs=in_specs,
        out_specs=out_specs,
        check_vma=False,
    )
```

```python
import math

import jax
import jax.numpy as jnp
from jax import lax
from jax.experimental import pallas as pl
from jax.experimental.pallas import tpu as pltpu
from jax.sharding import PartitionSpec as P

ROPE = 64
NOPE = 128
SCALE = (NOPE + ROPE) ** (-0.5)
NEG = -1e30
CHUNK = 1024
WIDE = 3072
AHEAD = 2
BF = jnp.bfloat16
F32 = jnp.float32
NT = (((1,), (1,)), ((), ()))
MESH = pl.DeviceIdType.MESH


def split3(x):
    hi = x.astype(BF).astype(F32)
    rest = x - hi
    mid = rest.astype(BF).astype(F32)
    return hi, mid, (rest - mid).astype(BF).astype(F32)


def farthest_first():
    hops = lambda o: sum(min(v, 4 - v) for v in o)
    offsets = [(y, x, z) for y in range(4) for x in range(4) for z in range(4)]
    return sorted(offsets, key=hops, reverse=True)[:-1]


def kernel(
    lengths,
    cache,
    queries,
    residual,
    value_up,
    out_w,
    gain,
    gate_w,
    up_w,
    down_w,
    hv_out,
    mix_out,
    kbuf,
    qbuf,
    sbuf,
    resbuf,
    vbuf,
    owbuf,
    gainbuf,
    gbuf,
    ubuf,
    dbuf,
    msg1,
    rcv1,
    x2,
    msg2,
    rcv2,
    stack,
    resid,
    msg3,
    rcv3,
    msg4,
    rcv4,
    wide,
    msg5,
    rcv5,
    msg6,
    rcv6,
    ksem,
    wsem,
    ssem,
    rsem,
):
    a = lax.axis_index("kva")
    b = lax.axis_index("kvb")
    requests, width, rows = kbuf.shape
    nq, heads = qbuf.shape[1], qbuf.shape[3]
    latent = vbuf.shape[1]
    qrows = nq * heads
    tokens = requests * nq
    d_model = owbuf.shape[1]
    tiles = d_model // 128
    chips = heads // 2
    pieces = latent // 128
    chunks = rows // CHUNK
    own = mix_out.shape[1]

    core = b % 2
    ys = [(a // 2 + k) % 4 for k in range(4)]
    xs = [((a % 2) * 2 + b // 8 + k) % 4 for k in range(4)]
    zs = [((b // 2) % 4 + k) % 4 for k in range(4)]
    chip = ys[0] * 16 + xs[0] * 4 + zs[0]
    y_part = [y * 2 for y in ys]
    x_part = [x // 2 for x in xs]
    x_low = [(x % 2) * 8 + core for x in xs]
    z_part = [z * 2 for z in zs]
    sibling = (a, b + 1 - 2 * core)

    def device_at(dy, dx, dz):
        return (y_part[dy] + x_part[dx], x_low[dx] + z_part[dz])

    def chip_at(dy, dx, dz):
        return ys[dy] * 16 + xs[dx] * 4 + zs[dz]

    offsets = farthest_first()

    qcopy = pltpu.make_async_copy(queries, qbuf, wsem.at[0])
    qcopy.start()
    kcopies = []
    for r in range(requests):
        for c in range(chunks):
            part = pl.ds(c * CHUNK, CHUNK)
            kcopies.append(
                pltpu.make_async_copy(
                    cache.at[r, :, part], kbuf.at[r, :, part], ksem.at[r * chunks + c]
                )
            )
    for copy in kcopies[:AHEAD]:
        copy.start()
    weights = [
        pltpu.make_async_copy(src, dst, wsem.at[i + 1])
        for i, (src, dst) in enumerate(
            (
                (value_up, vbuf),
                (residual, resbuf),
                (out_w, owbuf),
                (gain, gainbuf),
                (gate_w, gbuf),
                (up_w, ubuf),
                (down_w, dbuf),
            )
        )
    ]
    barrier = pltpu.get_barrier_semaphore()
    pl.semaphore_signal(barrier, inc=1, device_id=sibling, device_id_type=MESH)
    for off in offsets:
        pl.semaphore_signal(barrier, inc=1, device_id=device_at(*off), device_id_type=MESH)

    def send(stage, src, dst, device):
        pltpu.make_async_remote_copy(
            src_ref=src,
            dst_ref=dst,
            send_sem=ssem.at[stage],
            recv_sem=rsem.at[stage],
            device_id=device,
            device_id_type=MESH,
        ).start()

    def arrived(stage, buf):
        pltpu.make_async_copy(buf, buf, rsem.at[stage]).wait()

    def sent(stage, buf):
        pltpu.make_async_copy(buf, buf, ssem.at[stage]).wait()

    first = (a * 16 + b) * rows
    factor = SCALE * math.log2(math.e)

    def ordered(r, order):
        return jnp.concatenate(
            [
                lax.dot_general(order, qbuf[r, j], NT, preferred_element_type=F32).astype(BF)
                for j in range(nq)
            ],
            axis=0,
        )

    def scores(r, q):
        peak = None
        span = CHUNK if r == 0 else WIDE
        for c in range(rows // span):
            part = pl.ds(c * span, span)
            at = r * chunks + c * span // CHUNK
            for copy in kcopies[at : at + span // CHUNK]:
                copy.wait()
            if r == 0:
                kcopies[c + AHEAD].start()
            s = jnp.dot(q, kbuf[r, :, part], preferred_element_type=F32)
            pos = first + c * span + lax.broadcasted_iota(jnp.int32, (1, span), 1)
            halves = []
            for j in range(nq):
                bias = jnp.where(pos < lengths[r] - (nq - 1) + j, 0.0, NEG)
                halves.append(s[j * heads : (j + 1) * heads] + bias)
            s = jnp.concatenate(halves, axis=0)
            sbuf[:, part] = s
            for t in range(span // 128):
                tile = s[:, t * 128 : (t + 1) * 128]
                peak = tile if peak is None else jnp.maximum(peak, tile)
        return jnp.max(peak, axis=1, keepdims=True)

    def values(r, top):
        shift = top * factor
        total = jnp.zeros((qrows, 128), F32)
        numer = jnp.zeros((qrows, latent), F32)
        span = CHUNK if r == 0 else WIDE
        for c in range(rows // span):
            part = pl.ds(c * span, span)
            if r == 0 and c < chunks - AHEAD:
                kcopies[chunks + AHEAD + c].start()
            w = jnp.exp2(sbuf[:, part] * factor - shift)
            for t in range(span // 128):
                total = total + w[:, t * 128 : (t + 1) * 128]
            numer = numer + lax.dot_general(
                w.astype(BF), kbuf[r, :latent, part], NT, preferred_element_type=F32
            )
        total = jnp.sum(total, axis=1, keepdims=True)
        lse = top * SCALE + jnp.log(total)
        out = (numer * (1.0 / total)).astype(BF)
        lane = lax.broadcasted_iota(jnp.int32, (1, 128), 1)
        hi, mid, lo = split3(lse)
        tail = jnp.where(lane == 0, hi, jnp.where(lane == 1, mid, jnp.where(lane == 2, lo, 0.0)))
        tail = tail.astype(BF)
        for half in range(2):
            for j in range(nq):
                at = slice(j * heads + half * chips, j * heads + (half + 1) * chips)
                msg1[r, half, j, :, :latent] = out[at]
                msg1[r, half, j, :, latent:] = tail[at]
        if r == 0:
            pl.semaphore_wait(barrier, len(offsets) + 1)
        send(r, msg1.at[r, 1 - core], rcv1.at[r], sibling)

    def exchange(r):
        arrived(r, rcv1.at[r])
        for j in range(nq):
            parts = [msg1[r, core, j], rcv1[r, j]]
            vals = [x[:, :latent].astype(F32) for x in parts]
            lses = [jnp.sum(x[:, latent:].astype(F32), axis=1, keepdims=True) for x in parts]
            top = jnp.maximum(*lses)
            ws = [jnp.exp(x - top) for x in lses]
            den = ws[0] + ws[1]
            val = (ws[0] * vals[0] + ws[1] * vals[1]) * (1.0 / den)
            lse = top + jnp.log(den)
            for c in range(pieces):
                x2[:, c * nq + j, :] = val[:, c * 128 : (c + 1) * 128]
            for c, piece in enumerate(split3(jnp.broadcast_to(lse, (chips, 128)))):
                x2[:, (pieces + c) * nq + j, :] = piece
        msg2[r] = x2[...].astype(BF)
        for k, off in enumerate(offsets):
            send(2 + r, msg2.at[r, chip_at(*off)], rcv2.at[r, k], device_at(*off))

    def head_rows(r):
        arrived(2 + r, rcv2.at[r, pl.ds(0, len(offsets))])
        rcv2[r, len(offsets)] = msg2[r, chip]
        x = rcv2[r].astype(F32)
        edge = pieces * nq
        lse = (
            x[:, edge : edge + nq]
            + x[:, edge + nq : edge + 2 * nq]
            + x[:, edge + 2 * nq : edge + 3 * nq]
        )
        top = jnp.max(lse, axis=0, keepdims=True)
        w = jnp.exp(lse - top)
        w = w * (1.0 / jnp.sum(w, axis=0, keepdims=True))
        w = jnp.concatenate([w] * pieces, axis=1)
        att = jnp.sum(w * x[:, :edge], axis=0)
        total = jnp.zeros((nq, 128), F32)
        for c in range(pieces):
            total = total + jnp.dot(
                att[c * nq : (c + 1) * nq].astype(BF),
                vbuf[0, c * 128 : (c + 1) * 128, :],
                preferred_element_type=F32,
            )
        return total

    for c in range((pieces + 3) * nq, x2.shape[1]):
        x2[:, c, :] = jnp.zeros((chips, 128), F32)
    at = lax.broadcasted_iota(jnp.int32, (heads, heads), 0)
    head = lax.broadcasted_iota(jnp.int32, (heads, heads), 1)
    order = jnp.where(head == (at % chips) * 2 + at // chips, 1.0, 0.0).astype(BF)
    qcopy.wait()
    qs = [ordered(r, order) for r in range(requests)]
    values(0, scores(0, qs[0]))
    top = scores(1, qs[1])
    for copy in weights:
        copy.start()
    exchange(0)
    values(1, top)
    exchange(1)
    for copy in weights:
        copy.wait()
    for t in range(tiles):
        resid[t * tokens : (t + 1) * tokens, :] = resbuf[:, t * 128 : (t + 1) * 128].astype(F32)
    head_values = jnp.concatenate([head_rows(0), head_rows(1)], axis=0).astype(BF)
    hv_out[...] = head_values

    y = jnp.dot(head_values, owbuf[...], preferred_element_type=F32)
    for t in range(tiles):
        stack[t * tokens : (t + 1) * tokens, :] = y[:, t * 128 : (t + 1) * 128]
    msg3[...] = stack[...].astype(BF)
    send(4, msg3, rcv3, sibling)
    arrived(4, rcv3)
    summed = stack[...] + rcv3[...].astype(F32)
    lines = tiles * tokens
    third = (lines // 3 + 15) // 16 * 16
    for step in range(3):
        msg4[step] = summed.astype(BF)
        for k in (2, 1, 3):
            for g in range(3):
                part = pl.ds(g * third, min(third, lines - g * third))
                off = [0, 0, 0]
                off[(g + step) % 3] = k
                send(
                    5 + step,
                    msg4.at[step, part, :],
                    rcv4.at[step, k - 1, part, :],
                    device_at(*off),
                )
        arrived(5 + step, rcv4.at[step])
        for k in range(3):
            summed = summed + rcv4[step, k].astype(F32)
    stack[...] = (resid[...] + summed).astype(BF).astype(F32)
    for t in range(tiles):
        wide[:, t * 128 : (t + 1) * 128] = stack[t * tokens : (t + 1) * tokens, :]
    att = wide[...]
    mean_square = jnp.sum(att * att, axis=1, keepdims=True) / d_model
    normed = (
        att * lax.rsqrt(mean_square + 1e-06) * gainbuf[...].astype(F32).reshape(1, d_model)
    ).astype(BF)
    gate = lax.dot_general(normed, gbuf[...], NT, preferred_element_type=F32)
    up = lax.dot_general(normed, ubuf[...], NT, preferred_element_type=F32)
    hidden = (gate / (1.0 + jnp.exp(-gate)) * up).astype(BF)

    y = jnp.dot(hidden, dbuf[...], preferred_element_type=F32)
    y = y + jnp.where(chip * 2 + core == 0, att, 0.0)
    y = jnp.concatenate([y, jnp.zeros((tokens, 128), F32)], axis=1)
    for o in range(2 * chips):
        msg5[o % 2, o // 2] = y[:, o * own : o * own + 128]
    send(8, msg5.at[1 - core], rcv5, sibling)
    arrived(8, rcv5)
    msg6[...] = msg5[core] + rcv5[...]
    for k, off in enumerate(offsets):
        send(9, msg6.at[chip_at(*off)], rcv6.at[k], device_at(*off))
    arrived(9, rcv6)
    total = msg6[chip] + jnp.sum(rcv6[...], axis=0)
    mix_out[...] = total[:, :own].astype(BF)

    for r in range(requests):
        sent(r, rcv1.at[r])
        sent(2 + r, rcv2.at[r, pl.ds(0, len(offsets))])
    sent(4, rcv3)
    for step in range(3):
        sent(5 + step, rcv4.at[step])
    sent(8, rcv5)
    sent(9, rcv6)


def hand_on(head_values, mixed, head_values_out, mixed_out, sems):
    copies = [
        pltpu.make_async_copy(head_values, head_values_out, sems.at[0]),
        pltpu.make_async_copy(mixed, mixed_out, sems.at[1]),
    ]
    for copy in copies:
        copy.start()
    for copy in copies:
        copy.wait()


def per_device(
    latent_cache,
    lengths,
    queries,
    residual_in,
    value_up,
    out_weight,
    norm_gain,
    gate_weight,
    up_weight,
    down_weight,
):
    latent_cache = jnp.swapaxes(latent_cache, 1, 2)
    queries = jnp.swapaxes(queries, 2, 3)
    gate_weight = gate_weight.T
    up_weight = up_weight.T
    rows = latent_cache.shape[2]
    requests, nq, _, heads = queries.shape
    latent = value_up.shape[1]
    tokens, d_model = residual_in.shape
    chips = heads // 2
    lines = tokens * d_model // 128
    vmem = pltpu.VMEM
    scratch = [
        vmem(latent_cache.shape, BF),
        vmem(queries.shape, BF),
        vmem((nq * heads, rows), F32),
        vmem(residual_in.shape, BF),
        vmem(value_up.shape, BF),
        vmem(out_weight.shape, BF),
        vmem(norm_gain.shape, BF),
        vmem(gate_weight.shape, BF),
        vmem(up_weight.shape, BF),
        vmem(down_weight.shape, BF),
        vmem((requests, 2, nq, chips, latent + 128), BF),
        vmem((requests, nq, chips, latent + 128), BF),
        vmem((chips, 16, 128), F32),
        vmem((requests, chips, 16, 128), BF),
        vmem((requests, chips, 16, 128), BF),
        vmem((lines, 128), F32),
        vmem((lines, 128), F32),
        vmem((lines, 128), BF),
        vmem((lines, 128), BF),
        vmem((3, lines, 128), BF),
        vmem((3, 3, lines, 128), BF),
        vmem((tokens, d_model), F32),
        vmem((2, chips, tokens, 128), F32),
        vmem((chips, tokens, 128), F32),
        vmem((chips, tokens, 128), F32),
        vmem((chips - 1, tokens, 128), F32),
        pltpu.SemaphoreType.DMA((requests * (rows // CHUNK),)),
        pltpu.SemaphoreType.DMA((8,)),
        pltpu.SemaphoreType.DMA((10,)),
        pltpu.SemaphoreType.DMA((10,)),
    ]
    anywhere = pl.BlockSpec(memory_space=pl.ANY)
    results = pl.pallas_call(
        kernel,
        out_shape=(
            jax.ShapeDtypeStruct((tokens, value_up.shape[0] * value_up.shape[2]), BF),
            jax.ShapeDtypeStruct((tokens, d_model // heads), BF),
        ),
        in_specs=[pl.BlockSpec(memory_space=pltpu.SMEM)] + [anywhere] * 9,
        out_specs=(pl.BlockSpec(memory_space=pltpu.VMEM), pl.BlockSpec(memory_space=pltpu.VMEM)),
        scratch_shapes=scratch,
        compiler_params=pltpu.CompilerParams(
            collective_id=0, has_side_effects=True, vmem_limit_bytes=60 * 1024 * 1024
        ),
    )(
        lengths,
        latent_cache,
        queries,
        residual_in,
        value_up,
        out_weight,
        norm_gain,
        gate_weight,
        up_weight,
        down_weight,
    )
    return pl.pallas_call(
        hand_on,
        out_shape=tuple(jax.ShapeDtypeStruct(x.shape, x.dtype) for x in results),
        in_specs=[anywhere] * 2,
        out_specs=(anywhere,) * 2,
        scratch_shapes=[pltpu.SemaphoreType.DMA((2,))],
    )(*results)


def solution(mesh):
    both = ("kva", "kvb")
    in_specs = (
        P(None, both, None),
        P(),
        P(),
        P(),
        P(both, None, None),
        P(both, None),
        P(),
        P(None, both),
        P(None, both),
        P(both, None),
    )
    out_specs = (P(None, both), P(None, both))
    return jax.shard_map(
        per_device,
        mesh=mesh,
        in_specs=in_specs,
        out_specs=out_specs,
        check_vma=False,
    )
```
